32 devices in a mesh: lat: 8 (over z, y), lon: 4 (over x, core).
Axes of the slice: x: 2, y: 2, z: 4, core: 2. Of those that a mesh axis runs over, the one named last changes fastest.
Arguments:
- thermal_anomaly: float32 [32, 128, 512], P(None, 'lat', 'lon'), may hold values from -6 to 6
- moisture_ratio: float32 [32, 128, 512], P(None, 'lat', 'lon'), may hold values from 0.1 to 1
- zonal_cfl_ratio: float32 [32, 128, 512], P(None, 'lat', 'lon'), may hold values from -0.4 to 0.4
- meridional_cfl_ratio: float32 [32, 128, 512], P(None, 'lat', 'lon'), may hold values from -0.4 to 0.4
- lateral_smoothing_ratio: float32 [32, 128, 512], P(None, 'lat', 'lon'), may hold values from 0.1 to 0.2
- upright_smoothing_ratio: float32 [32, 128, 512], P(None, 'lat', 'lon'), may hold values from 0.3 to 3
- phase_choice: int32 [32, 128, 512], P(None, 'lat', 'lon'), may hold values 0 or 1
- physics_enabled_mask: int32 [128, 512], P('lat', 'lon'), may hold values from 0 to 1, as said below
- group_position_map: int32 [128, 512], P('lat', 'lon'), may hold values from 0 to 65535, as said below
Outputs:
- thermal_final: float32 [32, 128, 512], P(None, 'lat', 'lon')
- moisture_final: float32 [32, 128, 512], P(None, 'lat', 'lon')
- group_cloud_water: float32 [32, 2048], P(('lat', 'lon'))
The draws below stay inside these ranges and needn't reach their ends.
Inputs may be any that keep to these rules, and one draw needn't show every extreme that they name: `group_position_map`: every value appears once. A column's span is its value // 2048, held by the device of that index along lat+lon, at position value % 2048. Of the columns of one device exactly 32 go to each other device and 1056 stay on the device. `physics_enabled_mask`: every span holds exactly 768 active columns.
All inputs are finite; a program needn't handle non-finite values. No bound on the sum of `phase_choice` on one device may be relied on, other than what follows from the above.
Results may differ from the reference program's by a relative error of at most 0.000088.
Values sent between devices are 32-bit elements; how exact they have to be, the bound alone decides.
A program may use at most 64 MiB of HBM per device.

```python
import math
import jax
import jax.numpy as jnp
from jax import lax

STRATA_TOTAL = 32
LAT_DEV = 16
LON_DEV = 128
NDYN = 4
NSUB = 8
PARALLEL_CIRCLES = 128
MERIDIAN_TOTAL = 512
GROUP_WIDTH = 2048
N_LAT = 8
N_LON = 4


def span_layout(key):
    vertical_profile_set = LAT_DEV * LON_DEV
    devices = N_LAT * N_LON
    capacity = vertical_profile_set // (2 * devices)
    kept_count = vertical_profile_set // 2
    kept_active = vertical_profile_set // 8
    order_keys = jax.random.split(jax.random.fold_in(key, 11), devices)
    sequence_order = jax.vmap(lambda subkey: jax.random.permutation(subkey, vertical_profile_set))(order_keys)
    spot_keys = jax.random.split(jax.random.fold_in(key, 12), devices)
    spot_table = jax.vmap(lambda subkey: jax.random.permutation(subkey, vertical_profile_set))(spot_keys)
    sequence = jnp.arange(vertical_profile_set, dtype=jnp.int32)
    moving = sequence >= kept_count
    offset = jnp.maximum(sequence - kept_count, 0)
    group_index = offset // capacity
    within = offset % capacity
    source = jnp.arange(devices, dtype=jnp.int32)[:, None]
    target = jnp.where(moving[None, :], (source + group_index[None, :]) % devices, source)
    listed = jnp.where(moving, kept_count + group_index * capacity + within, sequence)
    position = spot_table[target, jnp.broadcast_to(listed[None, :], target.shape)]
    slot_seq = target * vertical_profile_set + position
    half_lon = N_LON // 2
    pair_share = jax.random.randint(jax.random.fold_in(key, 13), (N_LAT, half_lon), 0, capacity + 1)
    lat_index = source // N_LON
    lon_index = source % N_LON
    base_share = pair_share[lat_index, lon_index % half_lon]
    active_share = jnp.where(lon_index < half_lon, base_share, capacity - base_share)
    flag_seq = jnp.where(moving[None, :], within[None, :] < active_share, sequence[None, :] < kept_active).astype(jnp.int32)
    rows_index = jnp.broadcast_to(source, sequence_order.shape)
    slot_local = jnp.zeros((devices, vertical_profile_set), jnp.int32).at[rows_index, sequence_order].set(slot_seq)
    flag_local = jnp.zeros((devices, vertical_profile_set), jnp.int32).at[rows_index, sequence_order].set(flag_seq)

    def to_grid(values):
        return values.reshape(N_LAT, N_LON, LAT_DEV, LON_DEV).transpose(0, 2, 1, 3).reshape(N_LAT * LAT_DEV, N_LON * LON_DEV)
    return (to_grid(slot_local), to_grid(flag_local))


def draw_group_position_map(key, part):
    return span_layout(key)[0]


def draw_physics_enabled_mask(key, part):
    return span_layout(key)[1]


def place_ends(values, key, smallest, top_value):
    longest = values.shape.index(max(values.shape))
    spots = []
    for shift in (0, 1):
        where = [jax.random.randint(jax.random.fold_in(key, axis), (), 0, length) for axis, length in enumerate(values.shape)]
        where[longest] = (where[longest] + shift) % values.shape[longest]
        spots.append(tuple(where))
    return values.at[spots[0]].set(smallest).at[spots[1]].set(top_value)


def block_scale(stream_key, extent, cuts, least, top_value):
    def one(axis_at, shards_of):
        draws = jax.random.uniform(jax.random.fold_in(jax.random.fold_in(stream_key, 6), axis_at), (shards_of,), jnp.float32, least / len(cuts), top_value / len(cuts))
        return jnp.repeat(jnp.exp(draws), extent[axis_at] // shards_of).reshape((-1,) + (1,) * (len(extent) - axis_at - 1))

    loudness = one(*cuts[0])
    for cut in cuts[1:]:
        loudness = loudness * one(*cut)
    return loudness


def gaussian(stream_key, extent, spread, reach, pieces=(), kind=jnp.bfloat16):
    loudness = block_scale(stream_key, extent, pieces, -0.22, 0.18) if pieces else 1.0
    entries = jax.random.normal(stream_key, extent, jnp.float32) * spread * loudness
    return jnp.minimum(jnp.maximum(entries, -reach), reach).astype(kind)


def setup_inputs(seed: int = 0) -> dict:
    splits = jax.random.split(jax.random.key(seed), 10)
    thermal_anomaly = gaussian(splits[0], (STRATA_TOTAL, PARALLEL_CIRCLES, MERIDIAN_TOTAL), 1.0, 6.0, ((1, 8), (2, 4)), jnp.float32)
    moisture_ratio = jnp.clip(jnp.exp(math.log(1.0) - 2.3025851 * jax.random.uniform(splits[1], (STRATA_TOTAL, PARALLEL_CIRCLES, MERIDIAN_TOTAL), jnp.float32) ** block_scale(splits[1], (STRATA_TOTAL, PARALLEL_CIRCLES, MERIDIAN_TOTAL), ((1, 8), (2, 4)), -0.2, 0.2)), 0.1, 1.0)
    zonal_cfl_ratio = jnp.clip(jax.random.uniform(splits[2], (STRATA_TOTAL, PARALLEL_CIRCLES, MERIDIAN_TOTAL), jnp.float32, -0.4, 0.4) * block_scale(splits[2], (STRATA_TOTAL, PARALLEL_CIRCLES, MERIDIAN_TOTAL), ((1, 8), (2, 4)), -0.4, 0.0), -0.4, 0.4)
    meridional_cfl_ratio = jnp.clip(jax.random.uniform(splits[3], (STRATA_TOTAL, PARALLEL_CIRCLES, MERIDIAN_TOTAL), jnp.float32, -0.4, 0.4) * block_scale(splits[3], (STRATA_TOTAL, PARALLEL_CIRCLES, MERIDIAN_TOTAL), ((1, 8), (2, 4)), -0.4, 0.0), -0.4, 0.4)
    lateral_smoothing_ratio = jnp.clip(0.1 + 0.1 * jax.random.uniform(splits[4], (STRATA_TOTAL, PARALLEL_CIRCLES, MERIDIAN_TOTAL), jnp.float32) ** block_scale(splits[4], (STRATA_TOTAL, PARALLEL_CIRCLES, MERIDIAN_TOTAL), ((1, 8), (2, 4)), -0.2, 0.2), 0.1, 0.2)
    upright_smoothing_ratio = jnp.clip(jnp.exp(math.log(3.0) - 2.3025851 * jax.random.uniform(splits[5], (STRATA_TOTAL, PARALLEL_CIRCLES, MERIDIAN_TOTAL), jnp.float32) ** block_scale(splits[5], (STRATA_TOTAL, PARALLEL_CIRCLES, MERIDIAN_TOTAL), ((1, 8), (2, 4)), -0.2, 0.2)), 0.3, 3.0)
    phase_choice = place_ends((jax.random.randint(splits[6], (STRATA_TOTAL, PARALLEL_CIRCLES, MERIDIAN_TOTAL), 0, 2) < 1).astype(jnp.int32), jax.random.fold_in(splits[6], 1), 0, 1)
    physics_enabled_mask = draw_physics_enabled_mask(jax.random.fold_in(splits[9], 71), 0)
    group_position_map = draw_group_position_map(jax.random.fold_in(splits[9], 71), 0)
    return dict(thermal_anomaly=thermal_anomaly, moisture_ratio=moisture_ratio, zonal_cfl_ratio=zonal_cfl_ratio, meridional_cfl_ratio=meridional_cfl_ratio, lateral_smoothing_ratio=lateral_smoothing_ratio, upright_smoothing_ratio=upright_smoothing_ratio, phase_choice=phase_choice, physics_enabled_mask=physics_enabled_mask, group_position_map=group_position_map)


def cloud_process_step(temp_now, moist_now, branch_now, active_now):
    condensed = jnp.zeros_like(temp_now)
    for substep in range(NSUB):
        saturation = 0.5 * jnp.exp(0.25 * temp_now)
        excess = moist_now - saturation
        growth = 0.3 * jnp.maximum(excess, 0.0) / (1.0 + saturation)
        shrink = 0.15 * jnp.maximum(-excess, 0.0)
        change = jnp.where(branch_now > 0, growth, -shrink) * active_now
        moist_now = moist_now - change
        temp_now = temp_now + 2.0 * change
        condensed = condensed + change
    return temp_now, moist_now, jnp.sum(condensed, axis=0) * (4.0 / STRATA_TOTAL)


def column_solve(eddy_now, fields):
    strata_set = eddy_now.shape[0]
    upper_diag = eddy_now * (jnp.arange(strata_set) < strata_set - 1).astype(jnp.float32)[:, None]
    lower_diag = jnp.concatenate([jnp.zeros_like(upper_diag[:1]), upper_diag[:-1]], axis=0)
    middle_diag = 1.0 + lower_diag + upper_diag

    def forward(sweep_state, level_terms):
        sweep_ratio, sweep_value = sweep_state
        low_diag, main_diag, up_diag, right_side = level_terms
        pivot_value = main_diag - low_diag * sweep_ratio
        sweep_ratio = up_diag / pivot_value
        sweep_value = (right_side - low_diag * sweep_value) / pivot_value
        return (sweep_ratio, sweep_value), (sweep_ratio, sweep_value)

    initial = (jnp.zeros_like(eddy_now[0]), jnp.zeros_like(fields[:, 0]))
    final_state, stored = lax.scan(forward, initial, (lower_diag, middle_diag, upper_diag, jnp.moveaxis(fields, 1, 0)))

    def backward(next_level, level_terms):
        sweep_ratio, sweep_value = level_terms
        solved_level = sweep_value - sweep_ratio * next_level
        return solved_level, solved_level

    last_state, implicit_answer = lax.scan(backward, jnp.zeros_like(fields[:, 0]), stored, reverse=True)
    return jnp.moveaxis(implicit_answer, 0, 1)


def reference(thermal_anomaly, moisture_ratio, zonal_cfl_ratio, meridional_cfl_ratio, lateral_smoothing_ratio, upright_smoothing_ratio, phase_choice, physics_enabled_mask, group_position_map):
    east_face = 0.5 * (zonal_cfl_ratio + jnp.roll(zonal_cfl_ratio, -1, axis=2))
    east_mix = 0.5 * (lateral_smoothing_ratio + jnp.roll(lateral_smoothing_ratio, -1, axis=2))
    north_face = 0.5 * (meridional_cfl_ratio + jnp.roll(meridional_cfl_ratio, -1, axis=1))
    north_mix = 0.5 * (lateral_smoothing_ratio + jnp.roll(lateral_smoothing_ratio, -1, axis=1))
    pole_wall = (jnp.arange(PARALLEL_CIRCLES) < PARALLEL_CIRCLES - 1).astype(jnp.float32)[:, None]
    transported_quantities = jnp.stack([thermal_anomaly, moisture_ratio])
    for substep in range(NDYN):
        east_cell = jnp.roll(transported_quantities, -1, axis=3)
        flux_east = east_face * (0.5 * (transported_quantities + east_cell)) - east_mix * (east_cell - transported_quantities)
        north_cell = jnp.roll(transported_quantities, -1, axis=2)
        flux_north = (north_face * (0.5 * (transported_quantities + north_cell)) - north_mix * (north_cell - transported_quantities)) * pole_wall
        transported_quantities = transported_quantities - (flux_east - jnp.roll(flux_east, 1, axis=3)) - (flux_north - jnp.roll(flux_north, 1, axis=2))
    vertical_profile_set = PARALLEL_CIRCLES * MERIDIAN_TOTAL
    thermal_advected = transported_quantities[0].reshape(STRATA_TOTAL, vertical_profile_set)
    moisture_advected = transported_quantities[1].reshape(STRATA_TOTAL, vertical_profile_set)
    running_mask_linear = physics_enabled_mask.reshape(vertical_profile_set).astype(jnp.float32)
    heat_after_cloud, moisture_after_cloud, profile_rainfall = cloud_process_step(thermal_advected, moisture_advected, phase_choice.reshape(STRATA_TOTAL, vertical_profile_set), running_mask_linear)
    implicit_answer = column_solve(upright_smoothing_ratio.reshape(STRATA_TOTAL, vertical_profile_set), jnp.stack([heat_after_cloud, moisture_after_cloud]))
    thermal_rate_change = implicit_answer[0] - thermal_advected
    humid_tend = implicit_answer[1] - moisture_advected
    thermal_final = (thermal_advected + thermal_rate_change).reshape(STRATA_TOTAL, PARALLEL_CIRCLES, MERIDIAN_TOTAL)
    moisture_final = (moisture_advected + humid_tend).reshape(STRATA_TOTAL, PARALLEL_CIRCLES, MERIDIAN_TOTAL)
    assigned_profiles = jnp.zeros((vertical_profile_set,), jnp.float32).at[group_position_map.reshape(vertical_profile_set)].set(profile_rainfall)
    return thermal_final, moisture_final, assigned_profiles.reshape(vertical_profile_set // GROUP_WIDTH, GROUP_WIDTH)
```

```python
import functools

import jax
import jax.numpy as jnp
from jax import lax
from jax.experimental import pallas as pl
from jax.experimental.pallas import tpu as pltpu
from jax.sharding import PartitionSpec as P

NDYN = 4
NSUB = 8
GROUPS = 2
UNROLL = 4
MICRO = 4
MESH = pl.DeviceIdType.MESH
LOG2E = 1.4426950408889634
GAIN = 0.25 * LOG2E
NT = (((1,), (1,)), ((), ()))


def split3(x):
    high = x.astype(jnp.bfloat16)
    rest = x - high.astype(jnp.float32)
    mid = rest.astype(jnp.bfloat16)
    low = (rest - mid.astype(jnp.float32)).astype(jnp.bfloat16)
    return jnp.concatenate([high, mid, low], axis=0)


def join3(x):
    n = x.shape[0] // 3
    return x[:n] + x[n : 2 * n] + x[2 * n :]


def kernel(
    nlat,
    nlon,
    t_in,
    q_in,
    u_in,
    v_in,
    m_in,
    e_in,
    b_in,
    act_in,
    map_in,
    t_out,
    q_out,
    g_out,
    T,
    Q,
    C0,
    CE,
    CW,
    CN,
    CS,
    INV,
    RAT,
    col_to_east,
    col_to_west,
    col_from_west,
    col_from_east,
    row_to_north,
    row_to_south,
    row_from_south,
    row_from_north,
    onehot_t,
    onehot_r,
    onehot_lo,
    got_lo,
    pack2d,
    pos_out,
    pos_got,
    val_out,
    val_got,
    halo_send,
    halo_recv,
    pos_send,
    pos_recv,
    val_send,
    val_recv,
):
    levels, rows, cols = t_in.shape
    n = nlat * nlon
    width = rows * cols
    cap = width // (2 * n)
    per = cols // cap
    bundles = n // per
    glev = levels // GROUPS
    lat = lax.axis_index("lat")
    lon = lax.axis_index("lon")
    me = lat * nlon + lon
    east = lax.rem(lon + 1, nlon)
    west = lax.rem(lon + nlon - 1, nlon)
    north = lax.rem(lat + 1, nlat)
    south = lax.rem(lat + nlat - 1, nlat)
    has_north = lat < nlat - 1
    has_south = lat > 0

    def peer(i):
        d = lax.rem(me + 1 + i, n)
        return d, (d // nlon, lax.rem(d, nlon))

    barrier = pltpu.get_barrier_semaphore()

    @pl.loop(0, n - 1)
    def _(i):
        pl.semaphore_signal(barrier, inc=1, device_id=peer(i)[1], device_id_type=MESH)

    lane = lax.broadcasted_iota(jnp.int32, (rows, cols), 1)
    row = lax.broadcasted_iota(jnp.int32, (rows, cols), 0)

    def halo(kind, s, g):
        if kind == 0:
            src, dst, dev = col_to_east.at[s, g], col_from_west.at[s, g], (lat, east)
        elif kind == 1:
            src, dst, dev = col_to_west.at[s, g], col_from_east.at[s, g], (lat, west)
        else:
            a, b, y = (
                (row_to_north, row_from_south, north)
                if kind == 2
                else (row_to_south, row_from_north, south)
            )
            src, dst, dev = a.at[s, g], b.at[s, g], (y, lon)
            if s > 0:
                src, dst = a.at[s, g, pl.ds(0, 2)], b.at[s, g, pl.ds(0, 2)]
        return pltpu.make_async_remote_copy(
            src_ref=src,
            dst_ref=dst,
            send_sem=halo_send.at[kind, s, g],
            recv_sem=halo_recv.at[kind, s, g],
            device_id=dev,
            device_id_type=MESH,
        )

    def start_halos(s, g):
        pl.when(has_north)(lambda: halo(2, s, g).start())
        pl.when(has_south)(lambda: halo(3, s, g).start())
        halo(0, s, g).start()
        halo(1, s, g).start()

    def wait_halos(s, g):
        halo(0, s, g).wait_recv()
        halo(1, s, g).wait_recv()
        pl.when(has_south)(lambda: halo(2, s, g).wait_recv())
        pl.when(has_north)(lambda: halo(3, s, g).wait_recv())

    def end_halos(s, g):
        halo(0, s, g).wait_send()
        halo(1, s, g).wait_send()
        pl.when(has_north)(lambda: halo(2, s, g).wait_send())
        pl.when(has_south)(lambda: halo(3, s, g).wait_send())

    def put(x, which, k, s, g, l, acc):
        to_east, to_west = acc
        here = lane == which * levels + k
        to_east = jnp.where(here, x[:, cols - 1 : cols], to_east)
        to_west = jnp.where(here, x[:, 0:1], to_west)
        row_to_north[s, g, which, pl.ds(l, 1), :] = x[rows - 1 : rows, :]
        row_to_south[s, g, which, pl.ds(l, 1), :] = x[0:1, :]
        return to_east, to_west

    blank = jnp.zeros((rows, cols), jnp.float32)

    for g in range(GROUPS):

        def pack_body(i, acc, g=g):
            for j in range(UNROLL):
                l = i * UNROLL + j
                k = g * glev + l
                for which, ref in enumerate((t_in, q_in, m_in)):
                    acc = put(ref[k], which, k, 0, g, l, acc)
                to_east, to_west = acc
                x = u_in[k]
                here = lane == 3 * levels + k
                acc = (
                    jnp.where(here, x[:, cols - 1 : cols], to_east),
                    jnp.where(here, x[:, 0:1], to_west),
                )
                x = v_in[k]
                row_to_north[0, g, 3, pl.ds(l, 1), :] = x[rows - 1 : rows, :]
                row_to_south[0, g, 3, pl.ds(l, 1), :] = x[0:1, :]
            return acc

        to_east, to_west = lax.fori_loop(0, glev // UNROLL, pack_body, (blank, blank))
        col_to_east[0, g] = to_east
        col_to_west[0, g] = to_west

    @pl.when(jnp.logical_not(has_north))
    def _():
        row_from_north[...] = jnp.zeros_like(row_from_north)

    @pl.when(jnp.logical_not(has_south))
    def _():
        row_from_south[...] = jnp.zeros_like(row_from_south)

    pl.semaphore_wait(barrier, n - 1)
    for g in range(GROUPS):
        start_halos(0, g)

    shift = width.bit_length() - 1
    low_shift = cols.bit_length() - 1
    slot = map_in[...]
    target = lax.shift_right_logical(slot, shift)
    place = slot & (width - 1)
    place_hi = lax.shift_right_logical(place, low_shift)
    place_lo = place & (cols - 1)
    sub_n = lax.broadcasted_iota(jnp.int32, (n, cols), 0)
    sub_c = lax.broadcasted_iota(jnp.int32, (cols, cols), 0)
    lane_c = lax.broadcasted_iota(jnp.int32, (cols, cols), 1)
    before = (sub_c < lane_c).astype(jnp.bfloat16)
    offset = lax.rem(me, per) * cap
    base = jnp.zeros((n, 1), jnp.float32)
    packed_pos = jnp.zeros((2 * n, cols), jnp.float32)
    for r in range(rows):
        hit = (sub_n == target[r : r + 1, :]).astype(jnp.float32)
        onehot_t[r] = hit
        count = jnp.dot(
            hit.astype(jnp.bfloat16), before, preferred_element_type=jnp.float32
        )
        rank = jnp.sum(hit * (count + base), axis=0, keepdims=True).astype(jnp.int32)
        base = base + jnp.sum(hit, axis=1, keepdims=True)
        spread = (sub_c == rank + offset).astype(jnp.bfloat16)
        onehot_r[r] = spread
        onehot_lo[r] = (sub_c == place_lo[r : r + 1, :]).astype(jnp.bfloat16)
        marked = jnp.concatenate(
            [
                hit * place_hi[r : r + 1, :].astype(jnp.float32),
                hit * place_lo[r : r + 1, :].astype(jnp.float32),
            ],
            axis=0,
        ).astype(jnp.bfloat16)
        packed_pos = packed_pos + lax.dot_general(
            marked, spread, NT, preferred_element_type=jnp.float32
        )
    pack2d[...] = packed_pos[:n] * cols + packed_pos[n:]

    def pos_copy(i):
        d, dev = peer(i)
        return d, lambda slot_from: pltpu.make_async_remote_copy(
            src_ref=pos_out.at[d],
            dst_ref=pos_got.at[slot_from],
            send_sem=pos_send.at[d],
            recv_sem=pos_recv.at[slot_from],
            device_id=dev,
            device_id_type=MESH,
        )

    def val_copy(i):
        d, dev = peer(i)
        return d, lambda slot_from: pltpu.make_async_remote_copy(
            src_ref=val_out.at[d],
            dst_ref=val_got.at[slot_from],
            send_sem=val_send.at[d],
            recv_sem=val_recv.at[slot_from],
            device_id=dev,
            device_id_type=MESH,
        )

    @pl.loop(0, n - 1)
    def _(i):
        d, copy = pos_copy(i)
        pos_out[d] = pack2d[pl.ds(d, 1), :]
        copy(me).start()

    pos_got[me] = jnp.zeros((1, cols), jnp.float32)
    val_got[me] = jnp.zeros((1, cols), jnp.float32)

    def pivot_body(i, carry):
        below, ratio = carry
        for j in range(UNROLL):
            k = i * UNROLL + j
            above = jnp.where(k < levels - 1, e_in[k], 0.0)
            inverse = 1.0 / (1.0 + below + above - below * ratio)
            ratio = above * inverse
            INV[k] = inverse
            RAT[k] = ratio
            below = above
        return below, ratio

    lax.fori_loop(0, levels // UNROLL, pivot_body, (blank, blank))

    at_west = lane == 0
    at_east = lane == cols - 1
    at_south = row == 0
    at_north = row == rows - 1
    wall_n = jnp.where(
        jnp.logical_and(at_north, jnp.logical_not(has_north)), 0.0, 1.0
    )
    wall_s = jnp.where(
        jnp.logical_and(at_south, jnp.logical_not(has_south)), 0.0, 1.0
    )

    def from_west(x, packed, lane_from):
        moved = pltpu.roll(packed, lax.rem(cols - lane_from, cols), 1)
        return jnp.where(at_west, moved, pltpu.roll(x, 1, 1))

    def from_east(x, packed, lane_from):
        moved = pltpu.roll(packed, cols - 1 - lane_from, 1)
        return jnp.where(at_east, moved, pltpu.roll(x, cols - 1, 1))

    def from_south(x, edge):
        return jnp.where(at_south, edge, pltpu.roll(x, 1, 0))

    def from_north(x, edge):
        return jnp.where(at_north, edge, pltpu.roll(x, rows - 1, 0))

    def dynamics(s, g):
        wait_halos(s, g)
        packed_w = col_from_west[s, g]
        packed_e = col_from_east[s, g]

        def body(i, acc):
            for j in range(UNROLL):
                l = i * UNROLL + j
                k = g * glev + l

                def edge(ref, which):
                    return ref[s, g, which, pl.ds(l, 1), :]

                if s == 0:
                    u, v, m = u_in[k], v_in[k], m_in[k]
                    u_w = from_west(u, packed_w, 3 * levels + k)
                    u_e = from_east(u, packed_e, 3 * levels + k)
                    m_w = from_west(m, packed_w, 2 * levels + k)
                    m_e = from_east(m, packed_e, 2 * levels + k)
                    v_s = from_south(v, edge(row_from_south, 3))
                    v_n = from_north(v, edge(row_from_north, 3))
                    m_s = from_south(m, edge(row_from_south, 2))
                    m_n = from_north(m, edge(row_from_north, 2))
                    wind_e, mix_e = 0.25 * (u + u_e), 0.5 * (m + m_e)
                    wind_w, mix_w = 0.25 * (u_w + u), 0.5 * (m_w + m)
                    wind_n, mix_n = 0.25 * (v + v_n) * wall_n, 0.5 * (m + m_n) * wall_n
                    wind_s, mix_s = 0.25 * (v_s + v) * wall_s, 0.5 * (m_s + m) * wall_s
                    ce = mix_e - wind_e
                    cw = mix_w + wind_w
                    cn = mix_n - wind_n
                    cs = mix_s + wind_s
                    c0 = (
                        1.0
                        - (wind_e + mix_e)
                        + (wind_w - mix_w)
                        - (wind_n + mix_n)
                        + (wind_s - mix_s)
                    )
                    C0[k], CE[k], CW[k], CN[k], CS[k] = c0, ce, cw, cn, cs
                else:
                    c0, ce, cw, cn, cs = C0[k], CE[k], CW[k], CN[k], CS[k]
                for which, (source, held) in enumerate(((t_in, T), (q_in, Q))):
                    x = source[k] if s == 0 else held[k]
                    new = (
                        c0 * x
                        + ce * from_east(x, packed_e, which * levels + k)
                        + cw * from_west(x, packed_w, which * levels + k)
                    ) + (
                        cn * from_north(x, edge(row_from_north, which))
                        + cs * from_south(x, edge(row_from_south, which))
                    )
                    held[k] = new
                    if s < NDYN - 1:
                        acc = put(new, which, k, s + 1, g, l, acc)
            return acc

        to_east, to_west = lax.fori_loop(0, glev // UNROLL, body, (blank, blank))
        if s < NDYN - 1:
            col_to_east[s + 1, g] = to_east
            col_to_west[s + 1, g] = to_west
            start_halos(s + 1, g)

    active = act_in[...] > 0

    def micro(g, total):
        def body(i, total):
            first = g * glev + i * MICRO
            q0 = Q[pl.ds(first, MICRO)]
            t0 = T[pl.ds(first, MICRO)]
            branch = b_in[pl.ds(first, MICRO)] > 0
            grow = jnp.where(jnp.logical_and(active[None], branch), 0.3, 0.0)
            fade = jnp.where(jnp.logical_and(active[None], jnp.logical_not(branch)), 0.15, 0.0)
            start = GAIN * t0 - 1.0
            q = q0
            condensed = jnp.zeros_like(q0)
            for _ in range(NSUB):
                saturation = jnp.exp2(start + (2.0 * GAIN) * condensed)
                excess = q - saturation
                change = (grow * jnp.maximum(excess, 0.0)) / (1.0 + saturation) + (
                    fade * jnp.minimum(excess, 0.0)
                )
                q = q - change
                condensed = condensed + change
            Q[pl.ds(first, MICRO)] = q
            T[pl.ds(first, MICRO)] = t0 + 2.0 * condensed
            return total + jnp.sum(condensed, axis=0)

        return lax.fori_loop(0, glev // MICRO, body, total)

    for s in range(NDYN - 1):
        for g in range(GROUPS):
            dynamics(s, g)
    total = blank
    for g in range(GROUPS):
        dynamics(NDYN - 1, g)
        total = micro(g, total)
    precip = total * (4.0 / levels)

    packed = jnp.zeros((3 * n, cols), jnp.float32)
    for r in range(rows):
        packed = packed + lax.dot_general(
            split3(onehot_t[r] * precip[r : r + 1, :]),
            onehot_r[r],
            NT,
            preferred_element_type=jnp.float32,
        )
    pack2d[...] = join3(packed)

    @pl.loop(0, n - 1)
    def _(i):
        d, copy = val_copy(i)
        val_out[d] = pack2d[pl.ds(d, 1), :]
        copy(me).start()

    def forward(i, carry):
        below, t, q = carry
        for j in range(UNROLL):
            k = i * UNROLL + j
            inverse = INV[k]
            t = (T[k] - below * t) * inverse
            q = (Q[k] - below * q) * inverse
            T[k] = t
            Q[k] = q
            below = e_in[k]
        return below, t, q

    lax.fori_loop(0, levels // UNROLL, forward, (blank, blank, blank))

    def backward(i, carry):
        t, q = carry
        for j in range(UNROLL):
            k = levels - 1 - (i * UNROLL + j)
            ratio = RAT[k]
            t = T[k] - ratio * t
            q = Q[k] - ratio * q
            t_out[k] = t
            q_out[k] = q
        return t, q

    lax.fori_loop(0, levels // UNROLL, backward, (blank, blank))

    mine = target == me
    collected = jnp.zeros((3 * rows, cols), jnp.float32)
    for r in range(rows):
        keep = jnp.logical_and(mine[r : r + 1, :], row == place_hi[r : r + 1, :])
        collected = collected + lax.dot_general(
            split3(jnp.where(keep, precip[r : r + 1, :], 0.0)),
            onehot_lo[r],
            NT,
            preferred_element_type=jnp.float32,
        )

    @pl.loop(0, n - 1)
    def _(i):
        d, copy = pos_copy(i)
        copy(d).wait_recv()

    where_got = []
    for b in range(bundles):
        place_f = pos_got[b * per]
        for j in range(1, per):
            place_f = place_f + pos_got[b * per + j]
        place_b = place_f.astype(jnp.int32)
        where_got.append(lax.shift_right_logical(place_b, low_shift))
        got_lo[b] = (sub_c == (place_b & (cols - 1))).astype(jnp.bfloat16)

    @pl.loop(0, n - 1)
    def _(i):
        d, copy = val_copy(i)
        copy(d).wait_recv()

    for b in range(bundles):
        value = val_got[b * per]
        for j in range(1, per):
            value = value + val_got[b * per + j]
        collected = collected + lax.dot_general(
            split3(jnp.where(row == where_got[b], value, 0.0)),
            got_lo[b],
            NT,
            preferred_element_type=jnp.float32,
        )
    g_out[...] = join3(collected)

    for s in range(NDYN):
        for g in range(GROUPS):
            end_halos(s, g)

    @pl.loop(0, n - 1)
    def _(i):
        d, copy = pos_copy(i)
        copy(me).wait_send()
        d, copy = val_copy(i)
        copy(me).wait_send()


def on_device(t, q, u, v, m, e, b, act, slots):
    nlat = lax.axis_size("lat")
    nlon = lax.axis_size("lon")
    levels, rows, cols = t.shape
    n = nlat * nlon
    cap = rows * cols // (2 * n)
    bundles = n // (cols // cap)
    glev = levels // GROUPS
    f32 = jnp.float32
    field = pltpu.VMEM((levels, rows, cols), f32)
    column = pltpu.VMEM((NDYN, GROUPS, rows, cols), f32)
    strip = pltpu.VMEM((NDYN, GROUPS, 4, glev, cols), f32)
    packet = pltpu.VMEM((n, 1, cols), f32)
    vmem = pl.BlockSpec(memory_space=pltpu.VMEM)
    t_new, q_new, water = pl.pallas_call(
        functools.partial(kernel, nlat, nlon),
        out_shape=(
            jax.ShapeDtypeStruct(t.shape, f32),
            jax.ShapeDtypeStruct(t.shape, f32),
            jax.ShapeDtypeStruct((rows, cols), f32),
        ),
        in_specs=[vmem] * 9,
        out_specs=(vmem, vmem, vmem),
        scratch_shapes=[field] * 9
        + [column] * 4
        + [strip] * 4
        + [
            pltpu.VMEM((rows, n, cols), f32),
            pltpu.VMEM((rows, cols, cols), jnp.bfloat16),
            pltpu.VMEM((rows, cols, cols), jnp.bfloat16),
            pltpu.VMEM((bundles, cols, cols), jnp.bfloat16),
            pltpu.VMEM((n, cols), f32),
        ]
        + [packet] * 4
        + [pltpu.SemaphoreType.DMA((4, NDYN, GROUPS))] * 2
        + [pltpu.SemaphoreType.DMA((n,))] * 4,
        compiler_params=pltpu.CompilerParams(
            collective_id=0,
            has_side_effects=True,
            vmem_limit_bytes=48 * 1024 * 1024,
        ),
    )(t, q, u, v, m, e, b, act, slots)
    return t_new, q_new, water.reshape(1, rows * cols)


def solution(mesh):
    grid = P(None, "lat", "lon")
    flat = P("lat", "lon")
    return jax.shard_map(
        on_device,
        mesh=mesh,
        in_specs=(grid,) * 7 + (flat,) * 2,
        out_specs=(grid, grid, P(("lat", "lon"), None)),
        check_vma=False,
    )
```

```python
import functools

import jax
import jax.numpy as jnp
from jax import lax
from jax.experimental import pallas as pl
from jax.experimental.pallas import tpu as pltpu
from jax.sharding import PartitionSpec as P

NDYN = 4
NSUB = 8
GROUPS = 2
UNROLL = 2
MICRO = 4
SOLVE = 4
MESH = pl.DeviceIdType.MESH
LOG2E = 1.4426950408889634
GAIN = 0.25 * LOG2E
NT = (((1,), (1,)), ((), ()))


def split3(x):
    high = x.astype(jnp.bfloat16)
    rest = x - high.astype(jnp.float32)
    mid = rest.astype(jnp.bfloat16)
    low = (rest - mid.astype(jnp.float32)).astype(jnp.bfloat16)
    return jnp.concatenate([high, mid, low], axis=0)


def join3(x):
    n = x.shape[0] // 3
    return x[:n] + x[n : 2 * n] + x[2 * n :]


def kernel(
    nlat,
    nlon,
    levels,
    rows,
    t_hbm,
    q_hbm,
    u_hbm,
    v_hbm,
    m_hbm,
    e_hbm,
    b_hbm,
    act_hbm,
    map_hbm,
    t_out,
    q_out,
    g_out,
    t_in,
    q_in,
    u_in,
    v_in,
    m_in,
    e_in,
    b_in,
    act_in,
    map_in,
    load_sem,
    first,
    later,
    wind,
    C0,
    CE,
    CW,
    CN,
    CS,
    T,
    Q,
    INV,
    RAT,
    col_out,
    col_from_west,
    col_from_east,
    rain,
    onehot_t,
    onehot_r,
    onehot_lo,
    pack2d,
    packet_out,
    packet_got,
    halo_send,
    halo_recv,
    packet_send,
    packet_recv,
):
    cols = t_hbm.shape[1]
    n = nlat * nlon
    width = rows * cols
    cap = width // (2 * n)
    per = cols // cap
    bundles = n // per
    glev = levels // GROUPS
    lat = lax.axis_index("lat")
    lon = lax.axis_index("lon")
    me = lat * nlon + lon
    east = lax.rem(lon + 1, nlon)
    west = lax.rem(lon + nlon - 1, nlon)
    north = lax.rem(lat + 1, nlat)
    south = lax.rem(lat + nlat - 1, nlat)
    has_north = lat < nlat - 1
    has_south = lat > 0

    def peer(i):
        d = lax.rem(me + 1 + i, n)
        return d, (d // nlon, lax.rem(d, nlon))

    loads = {}
    for i, (source, held) in enumerate(
        (
            (t_hbm, t_in),
            (q_hbm, q_in),
            (m_hbm, m_in),
            (u_hbm, u_in),
            (v_hbm, v_in),
            (map_hbm, map_in),
            (e_hbm, e_in),
            (act_hbm, act_in),
            (b_hbm, b_in),
        )
    ):
        loads[i] = pltpu.make_async_copy(source, held, load_sem.at[i])
        loads[i].start()

    barrier = pltpu.get_barrier_semaphore()

    @pl.loop(0, n - 1)
    def _(i):
        pl.semaphore_signal(barrier, inc=1, device_id=peer(i)[1], device_id_type=MESH)

    def state(s, which):
        return first.at[which] if s == 0 else later.at[s - 1, which]

    def halo(kind, s, g):
        part = pl.ds(g * glev, glev)
        if kind == 0:
            src, dst, dev = col_out.at[s, g], col_from_west.at[s, g], (lat, east)
        elif kind == 1:
            src, dst, dev = col_out.at[s, g], col_from_east.at[s, g], (lat, west)
        else:
            ref = first if s == 0 else later.at[s - 1]
            source, target, y = (rows, 0, north) if kind == 2 else (1, rows + 1, south)
            src, dst, dev = ref.at[:, source, part], ref.at[:, target, part], (y, lon)
        return pltpu.make_async_remote_copy(
            src_ref=src,
            dst_ref=dst,
            send_sem=halo_send.at[kind, s, g],
            recv_sem=halo_recv.at[kind, s, g],
            device_id=dev,
            device_id_type=MESH,
        )

    def start_halos(s, g):
        pl.when(has_north)(lambda: halo(2, s, g).start())
        pl.when(has_south)(lambda: halo(3, s, g).start())
        halo(0, s, g).start()
        halo(1, s, g).start()

    def wait_halos(s, g):
        halo(0, s, g).wait_recv()
        halo(1, s, g).wait_recv()
        pl.when(has_south)(lambda: halo(2, s, g).wait_recv())
        pl.when(has_north)(lambda: halo(3, s, g).wait_recv())

    def end_halos(s, g):
        halo(0, s, g).wait_send()
        halo(1, s, g).wait_send()
        pl.when(has_north)(lambda: halo(2, s, g).wait_send())
        pl.when(has_south)(lambda: halo(3, s, g).wait_send())

    lane = lax.broadcasted_iota(jnp.int32, (glev, cols), 1)
    pair = (lane + 1) // 2
    pair = jnp.where(lane == cols - 1, 0, pair)
    at_west = lane == 0
    at_east = lane == cols - 1

    def put(x, p, packed):
        return jnp.where(pair == p, pltpu.roll(x, 2 * p, 1), packed)

    blank = jnp.zeros((glev, cols), jnp.float32)

    @pl.when(jnp.logical_not(has_north))
    def _():
        first[:, rows + 1] = jnp.zeros_like(first[:, rows + 1])
        later[:, :, rows + 1] = jnp.zeros_like(later[:, :, rows + 1])

    @pl.when(jnp.logical_not(has_south))
    def _():
        first[:, 0] = jnp.zeros_like(first[:, 0])
        later[:, :, 0] = jnp.zeros_like(later[:, :, 0])

    for i in range(5):
        loads[i].wait()

    for g in range(GROUPS):

        def arrange(i, packed, g=g):
            for j in range(UNROLL):
                r = i * UNROLL + j
                spots = pl.ds(g * glev * rows + r, glev, rows)
                part = pl.ds(g * glev, glev)
                for which, ref in enumerate((t_in, q_in, m_in)):
                    x = ref[spots, :]
                    first[which, r + 1, part] = x
                    packed = put(x, which * rows + r, packed)
                x = u_in[spots, :]
                wind[r, part] = x
                packed = put(x, 3 * rows + r, packed)
                first[3, r + 1, part] = v_in[spots, :]
            return packed

        col_out[0, g] = lax.fori_loop(0, rows // UNROLL, arrange, blank)

    loads[6].wait()
    plane = jnp.zeros((rows, cols), jnp.float32)

    def level(k):
        return pl.ds(pl.multiple_of(k * rows, rows), rows)

    def pivot_body(i, carry):
        below, ratio = carry
        for j in range(SOLVE):
            k = i * SOLVE + j
            above = jnp.where(k < levels - 1, e_in[level(k), :], 0.0)
            inverse = 1.0 / (1.0 + below + above - below * ratio)
            ratio = above * inverse
            INV[level(k), :] = inverse
            RAT[level(k), :] = ratio
            below = above
        return below, ratio

    def pivots():
        lax.fori_loop(0, levels // SOLVE, pivot_body, (plane, plane))

    loads[5].wait()
    shift = width.bit_length() - 1
    low_shift = cols.bit_length() - 1
    slot = map_in[...]
    target = lax.shift_right_logical(slot, shift)
    place = slot & (width - 1)
    place_hi = lax.shift_right_logical(place, low_shift)
    place_lo = place & (cols - 1)
    sub_n = lax.broadcasted_iota(jnp.int32, (n, cols), 0)
    sub_c = lax.broadcasted_iota(jnp.int32, (cols, cols), 0)
    sub_r = lax.broadcasted_iota(jnp.int32, (rows, cols), 0)
    lane_c = lax.broadcasted_iota(jnp.int32, (cols, cols), 1)
    before = (sub_c < lane_c).astype(jnp.bfloat16)
    offset = lax.rem(me, per) * cap

    def slots(some, carry):
        base, packed_pos = carry
        for r in some:
            hit = (sub_n == target[r : r + 1, :]).astype(jnp.float32)
            onehot_t[r] = hit
            count = jnp.dot(
                hit.astype(jnp.bfloat16), before, preferred_element_type=jnp.float32
            )
            rank = jnp.sum(hit * (count + base), axis=0, keepdims=True).astype(jnp.int32)
            base = base + jnp.sum(hit, axis=1, keepdims=True)
            spread = (sub_c == rank + offset).astype(jnp.bfloat16)
            onehot_r[r] = spread
            onehot_lo[r] = (sub_c == place_lo[r : r + 1, :]).astype(jnp.bfloat16)
            marked = jnp.concatenate(
                [
                    hit * place_hi[r : r + 1, :].astype(jnp.float32),
                    hit * place_lo[r : r + 1, :].astype(jnp.float32),
                ],
                axis=0,
            ).astype(jnp.bfloat16)
            packed_pos = packed_pos + lax.dot_general(
                marked, spread, NT, preferred_element_type=jnp.float32
            )
        return base, packed_pos

    quarter = rows // 4
    sorting = (jnp.zeros((n, 1), jnp.float32), jnp.zeros((2 * n, cols), jnp.float32))
    pivots()
    pl.semaphore_wait(barrier, n - 1)
    for g in range(GROUPS):
        start_halos(0, g)
    sorting = slots(range(quarter), sorting)

    def dynamics(s, g):
        wait_halos(s, g)
        even = lax.rem(lane, 2) == 0
        edges = jnp.where(
            even,
            pltpu.roll(col_from_west[s, g], 1, 1),
            pltpu.roll(col_from_east[s, g], cols - 1, 1),
        )
        part = pl.ds(g * glev, glev)

        def sides(x, p):
            edge = pltpu.roll(edges, lax.rem(cols - 2 * p, cols), 1)
            return (
                jnp.where(at_west, edge, pltpu.roll(x, 1, 1)),
                jnp.where(at_east, edge, pltpu.roll(x, cols - 1, 1)),
            )

        def body(i, packed):
            for j in range(UNROLL):
                r = i * UNROLL + j
                if s == 0:
                    wall_n = jnp.where(
                        jnp.logical_and(r == rows - 1, jnp.logical_not(has_north)), 0.0, 1.0
                    )
                    wall_s = jnp.where(
                        jnp.logical_and(r == 0, jnp.logical_not(has_south)), 0.0, 1.0
                    )
                    m = first[2, r + 1, part]
                    m_s = first[2, r, part]
                    m_n = first[2, r + 2, part]
                    v = first[3, r + 1, part]
                    v_s = first[3, r, part]
                    v_n = first[3, r + 2, part]
                    u = wind[r, part]
                    u_w, u_e = sides(u, 3 * rows + r)
                    m_w, m_e = sides(m, 2 * rows + r)
                    wind_e, mix_e = 0.25 * (u + u_e), 0.5 * (m + m_e)
                    wind_w, mix_w = 0.25 * (u_w + u), 0.5 * (m_w + m)
                    wind_n, mix_n = 0.25 * (v + v_n) * wall_n, 0.5 * (m + m_n) * wall_n
                    wind_s, mix_s = 0.25 * (v_s + v) * wall_s, 0.5 * (m_s + m) * wall_s
                    ce = mix_e - wind_e
                    cw = mix_w + wind_w
                    cn = mix_n - wind_n
                    cs = mix_s + wind_s
                    c0 = (
                        1.0
                        - (wind_e + mix_e)
                        + (wind_w - mix_w)
                        - (wind_n + mix_n)
                        + (wind_s - mix_s)
                    )
                    C0[r, part] = c0
                    CE[r, part] = ce
                    CW[r, part] = cw
                    CN[r, part] = cn
                    CS[r, part] = cs
                else:
                    c0 = C0[r, part]
                    ce = CE[r, part]
                    cw = CW[r, part]
                    cn = CN[r, part]
                    cs = CS[r, part]
                for which in range(2):
                    ref = state(s, which)
                    x = ref[r + 1, part]
                    x_w, x_e = sides(x, which * rows + r)
                    new = (c0 * x + ce * x_e + cw * x_w) + (
                        cn * ref[r + 2, part] + cs * ref[r, part]
                    )
                    if s < NDYN - 1:
                        later[s, which, r + 1, part] = new
                        packed = put(new, which * rows + r, packed)
                    else:
                        (T, Q)[which][pl.ds(pl.multiple_of(r * levels + g * glev, 8), glev), :] = new
            return packed

        packed = lax.fori_loop(0, rows // UNROLL, body, blank)
        if s < NDYN - 1:
            col_out[s + 1, g] = packed
            start_halos(s + 1, g)

    loads[7].wait()
    loads[8].wait()

    def micro(g):
        def body(i, carry):
            for j in range(MICRO // 2):
                r = i * (MICRO // 2) + j
                spots = pl.ds(pl.multiple_of(r * levels + g * glev, 8), glev)
                q0 = Q[spots, :]
                t0 = T[spots, :]
                branch = b_in[pl.ds(g * glev * rows + r, glev, rows), :] > 0
                active = act_in[pl.ds(r, 1), :] > 0
                grow = jnp.where(jnp.logical_and(active, branch), 0.3, 0.0)
                fade = jnp.where(jnp.logical_and(active, jnp.logical_not(branch)), 0.15, 0.0)
                start = GAIN * t0 - 1.0
                q = q0
                condensed = jnp.zeros_like(q0)
                for _ in range(NSUB):
                    saturation = jnp.exp2(start + (2.0 * GAIN) * condensed)
                    excess = q - saturation
                    change = (grow * jnp.maximum(excess, 0.0)) / (1.0 + saturation) + (
                        fade * jnp.minimum(excess, 0.0)
                    )
                    q = q - change
                    condensed = condensed + change
                Q[spots, :] = q
                T[spots, :] = t0 + 2.0 * condensed
                rain[g, pl.ds(r, 1), :] = jnp.sum(condensed, axis=0, keepdims=True)
            return carry

        lax.fori_loop(0, rows // (MICRO // 2), body, 0)

    for s in range(NDYN - 1):
        for g in range(GROUPS):
            dynamics(s, g)
        sorting = slots(range((s + 1) * quarter, (s + 2) * quarter), sorting)
    packed_pos = sorting[1]
    pack2d[:n] = packed_pos[:n] * cols + packed_pos[n:]
    for g in range(GROUPS):
        dynamics(NDYN - 1, g)
        micro(g)
    precip = jnp.sum(rain[...], axis=0) * (4.0 / levels)

    packed = jnp.zeros((3 * n, cols), jnp.float32)
    for r in range(rows):
        packed = packed + lax.dot_general(
            split3(onehot_t[r] * precip[r : r + 1, :]),
            onehot_r[r],
            NT,
            preferred_element_type=jnp.float32,
        )
    pack2d[n:] = join3(packed)

    def packet(i):
        d, dev = peer(i)
        return d, pltpu.make_async_remote_copy(
            src_ref=packet_out.at[d],
            dst_ref=packet_got.at[me],
            send_sem=packet_send.at[d],
            recv_sem=packet_recv.at[me],
            device_id=dev,
            device_id_type=MESH,
        )

    @pl.loop(0, n - 1)
    def _(i):
        d, copy = packet(i)
        packet_out[d, 0:1] = pack2d[pl.ds(d, 1), :]
        packet_out[d, 1:2] = pack2d[pl.ds(n + d, 1), :]
        copy.start()

    packet_got[me] = jnp.zeros(packet_got.shape[1:], jnp.float32)

    def forward(i, carry):
        below, t, q = carry
        for j in range(SOLVE):
            k = i * SOLVE + j
            inverse = INV[level(k), :]
            t = (T[pl.ds(k, rows, levels), :] - below * t) * inverse
            q = (Q[pl.ds(k, rows, levels), :] - below * q) * inverse
            t_in[level(k), :] = t
            q_in[level(k), :] = q
            below = e_in[level(k), :]
        return below, t, q

    lax.fori_loop(0, levels // SOLVE, forward, (plane, plane, plane))

    def backward(i, carry):
        t, q = carry
        for j in range(SOLVE):
            k = levels - 1 - (i * SOLVE + j)
            ratio = RAT[level(k), :]
            t = t_in[level(k), :] - ratio * t
            q = q_in[level(k), :] - ratio * q
            t_out[level(k), :] = t
            q_out[level(k), :] = q
        return t, q

    lax.fori_loop(0, levels // SOLVE, backward, (plane, plane))

    mine = target == me
    collected = jnp.zeros((3 * rows, cols), jnp.float32)
    for r in range(rows):
        keep = jnp.logical_and(mine[r : r + 1, :], sub_r == place_hi[r : r + 1, :])
        collected = collected + lax.dot_general(
            split3(jnp.where(keep, precip[r : r + 1, :], 0.0)),
            onehot_lo[r],
            NT,
            preferred_element_type=jnp.float32,
        )

    @pl.loop(0, n - 1)
    def _(i):
        d = peer(i)[0]
        pltpu.make_async_copy(packet_got.at[d], packet_got.at[d], packet_recv.at[d]).wait()

    for b in range(bundles):
        both = packet_got[b * per]
        for j in range(1, per):
            both = both + packet_got[b * per + j]
        place_b = both[0:1].astype(jnp.int32)
        got_hi = lax.shift_right_logical(place_b, low_shift)
        got_low = (sub_c == (place_b & (cols - 1))).astype(jnp.bfloat16)
        collected = collected + lax.dot_general(
            split3(jnp.where(sub_r == got_hi, both[1:2], 0.0)),
            got_low,
            NT,
            preferred_element_type=jnp.float32,
        )
    g_out[...] = join3(collected)

    for s in range(NDYN):
        for g in range(GROUPS):
            end_halos(s, g)

    @pl.loop(0, n - 1)
    def _(i):
        packet(i)[1].wait_send()


def on_device(t, q, u, v, m, e, b, act, slots):
    nlat = lax.axis_size("lat")
    nlon = lax.axis_size("lon")
    levels, rows, cols = t.shape
    n = nlat * nlon
    glev = levels // GROUPS
    f32 = jnp.float32
    flat = pltpu.VMEM((levels * rows, cols), f32)
    field = pltpu.VMEM((rows, levels, cols), f32)
    column = pltpu.VMEM((NDYN, GROUPS, glev, cols), f32)
    vmem = pl.BlockSpec(memory_space=pltpu.VMEM)
    t_new, q_new, water = pl.pallas_call(
        functools.partial(kernel, nlat, nlon, levels, rows),
        out_shape=(
            jax.ShapeDtypeStruct((levels * rows, cols), f32),
            jax.ShapeDtypeStruct((levels * rows, cols), f32),
            jax.ShapeDtypeStruct((rows, cols), f32),
        ),
        in_specs=[pl.BlockSpec(memory_space=pltpu.HBM)] * 9,
        out_specs=(vmem, vmem, vmem),
        scratch_shapes=[flat] * 6
        + [pltpu.VMEM((levels * rows, cols), jnp.int32)]
        + [pltpu.VMEM((rows, cols), jnp.int32)] * 2
        + [pltpu.SemaphoreType.DMA((9,))]
        + [
            pltpu.VMEM((4, rows + 2, levels, cols), f32),
            pltpu.VMEM((NDYN - 1, 2, rows + 2, levels, cols), f32),
        ]
        + [field] * 6
        + [flat] * 4
        + [column] * 3
        + [
            pltpu.VMEM((GROUPS, rows, cols), f32),
            pltpu.VMEM((rows, n, cols), f32),
            pltpu.VMEM((rows, cols, cols), jnp.bfloat16),
            pltpu.VMEM((rows, cols, cols), jnp.bfloat16),
            pltpu.VMEM((2 * n, cols), f32),
            pltpu.VMEM((n, 2, cols), f32),
            pltpu.VMEM((n, 2, cols), f32),
        ]
        + [pltpu.SemaphoreType.DMA((4, NDYN, GROUPS))] * 2
        + [pltpu.SemaphoreType.DMA((n,))] * 2,
        compiler_params=pltpu.CompilerParams(collective_id=0, has_side_effects=True),
    )(*(x.reshape(levels * rows, cols) for x in (t, q, u, v, m, e, b)), act, slots)
    return t_new.reshape(t.shape), q_new.reshape(t.shape), water.reshape(1, rows * cols)


def solution(mesh):
    grid = P(None, "lat", "lon")
    flat = P("lat", "lon")
    return jax.shard_map(
        on_device,
        mesh=mesh,
        in_specs=(grid,) * 7 + (flat,) * 2,
        out_specs=(grid, grid, P(("lat", "lon"), None)),
        check_vma=False,
    )
```

```python
import functools

import jax
import jax.numpy as jnp
from jax import lax
from jax.experimental import pallas as pl
from jax.experimental.pallas import tpu as pltpu
from jax.sharding import PartitionSpec as P

NDYN = 4
NSUB = 8
GROUPS = 2
UNROLL = 4
MICRO = 8
SOLVE = 8
MESH = pl.DeviceIdType.MESH
LOG2E = 1.4426950408889634
GAIN = 0.25 * LOG2E
NT = (((1,), (1,)), ((), ()))


def split3(x):
    high = x.astype(jnp.bfloat16)
    rest = x - high.astype(jnp.float32)
    mid = rest.astype(jnp.bfloat16)
    low = (rest - mid.astype(jnp.float32)).astype(jnp.bfloat16)
    return jnp.concatenate([high, mid, low], axis=0)


def join3(x):
    n = x.shape[0] // 3
    return x[:n] + x[n : 2 * n] + x[2 * n :]


def kernel(
    nlat,
    nlon,
    levels,
    rows,
    t_hbm,
    q_hbm,
    u_hbm,
    v_hbm,
    m_hbm,
    e_hbm,
    b_hbm,
    act_hbm,
    map_hbm,
    t_out,
    q_out,
    g_out,
    t_in,
    q_in,
    u_in,
    v_in,
    m_in,
    e_in,
    b_in,
    act_in,
    map_in,
    load_sem,
    first,
    later,
    wind,
    C0,
    CE,
    CW,
    CN,
    CS,
    T,
    Q,
    INV,
    RAT,
    col_out,
    col_from_west,
    col_from_east,
    rain,
    onehot_t,
    onehot_r,
    onehot_lo,
    pack2d,
    packet_out,
    packet_got,
    halo_send,
    halo_recv,
    packet_send,
    packet_recv,
):
    cols = t_hbm.shape[1]
    n = nlat * nlon
    width = rows * cols
    cap = width // (2 * n)
    per = cols // cap
    bundles = n // per
    glev = levels // GROUPS
    lat = lax.axis_index("lat")
    lon = lax.axis_index("lon")
    me = lat * nlon + lon
    east = lax.rem(lon + 1, nlon)
    west = lax.rem(lon + nlon - 1, nlon)
    north = lax.rem(lat + 1, nlat)
    south = lax.rem(lat + nlat - 1, nlat)
    has_north = lat < nlat - 1
    has_south = lat > 0

    def peer(i):
        d = lax.rem(me + 1 + i, n)
        return d, (d // nlon, lax.rem(d, nlon))

    loads = {}
    for i, (source, held) in enumerate(
        (
            (t_hbm, t_in),
            (q_hbm, q_in),
            (m_hbm, m_in),
            (u_hbm, u_in),
            (v_hbm, v_in),
            (map_hbm, map_in),
            (e_hbm, e_in),
            (act_hbm, act_in),
            (b_hbm, b_in),
        )
    ):
        loads[i] = pltpu.make_async_copy(source, held, load_sem.at[i])
        loads[i].start()

    barrier = pltpu.get_barrier_semaphore()

    @pl.loop(0, n - 1)
    def _(i):
        pl.semaphore_signal(barrier, inc=1, device_id=peer(i)[1], device_id_type=MESH)

    def state(s, which):
        return first.at[which] if s == 0 else later.at[s - 1, which]

    def halo(kind, s, g):
        part = pl.ds(g * glev, glev)
        if kind == 0:
            src, dst, dev = col_out.at[s, g], col_from_west.at[s, g], (lat, east)
        elif kind == 1:
            src, dst, dev = col_out.at[s, g], col_from_east.at[s, g], (lat, west)
        else:
            ref = first if s == 0 else later.at[s - 1]
            source, target, y = (rows, 0, north) if kind == 2 else (1, rows + 1, south)
            src, dst, dev = ref.at[:, source, part], ref.at[:, target, part], (y, lon)
        return pltpu.make_async_remote_copy(
            src_ref=src,
            dst_ref=dst,
            send_sem=halo_send.at[kind, s, g],
            recv_sem=halo_recv.at[kind, s, g],
            device_id=dev,
            device_id_type=MESH,
        )

    def start_halos(s, g):
        pl.when(has_north)(lambda: halo(2, s, g).start())
        pl.when(has_south)(lambda: halo(3, s, g).start())
        halo(0, s, g).start()
        halo(1, s, g).start()

    def wait_halos(s, g):
        halo(0, s, g).wait_recv()
        halo(1, s, g).wait_recv()
        pl.when(has_south)(lambda: halo(2, s, g).wait_recv())
        pl.when(has_north)(lambda: halo(3, s, g).wait_recv())

    def end_halos(s, g):
        halo(0, s, g).wait_send()
        halo(1, s, g).wait_send()
        pl.when(has_north)(lambda: halo(2, s, g).wait_send())
        pl.when(has_south)(lambda: halo(3, s, g).wait_send())

    lane = lax.broadcasted_iota(jnp.int32, (glev, cols), 1)
    pair = (lane + 1) // 2
    pair = jnp.where(lane == cols - 1, 0, pair)
    at_west = lane == 0
    at_east = lane == cols - 1

    def put(x, p, packed):
        return jnp.where(pair == p, pltpu.roll(x, 2 * p, 1), packed)

    blank = jnp.zeros((glev, cols), jnp.float32)

    @pl.when(jnp.logical_not(has_north))
    def _():
        first[:, rows + 1] = jnp.zeros_like(first[:, rows + 1])
        later[:, :, rows + 1] = jnp.zeros_like(later[:, :, rows + 1])

    @pl.when(jnp.logical_not(has_south))
    def _():
        first[:, 0] = jnp.zeros_like(first[:, 0])
        later[:, :, 0] = jnp.zeros_like(later[:, :, 0])

    for i in range(5):
        loads[i].wait()

    for g in range(GROUPS):

        def arrange(i, packed, g=g):
            for j in range(UNROLL):
                r = i * UNROLL + j
                spots = pl.ds(g * glev * rows + r, glev, rows)
                part = pl.ds(g * glev, glev)
                for which, ref in enumerate((t_in, q_in, m_in)):
                    x = ref[spots, :]
                    first[which, r + 1, part] = x
                    packed = put(x, which * rows + r, packed)
                x = u_in[spots, :]
                wind[r, part] = x
                packed = put(x, 3 * rows + r, packed)
                first[3, r + 1, part] = v_in[spots, :]
            return packed

        col_out[0, g] = lax.fori_loop(0, rows // UNROLL, arrange, blank)

    loads[6].wait()
    plane = jnp.zeros((rows, cols), jnp.float32)

    def level(k):
        return pl.ds(pl.multiple_of(k * rows, rows), rows)

    def pivot_body(i, carry):
        below, ratio = carry
        for j in range(SOLVE):
            k = i * SOLVE + j
            above = jnp.where(k < levels - 1, e_in[level(k), :], 0.0)
            inverse = 1.0 / (1.0 + below + above - below * ratio)
            ratio = above * inverse
            INV[level(k), :] = inverse
            RAT[level(k), :] = ratio
            below = above
        return below, ratio

    def pivots():
        lax.fori_loop(0, levels // SOLVE, pivot_body, (plane, plane))

    loads[5].wait()
    shift = width.bit_length() - 1
    low_shift = cols.bit_length() - 1
    slot = map_in[...]
    target = lax.shift_right_logical(slot, shift)
    place = slot & (width - 1)
    place_hi = lax.shift_right_logical(place, low_shift)
    place_lo = place & (cols - 1)
    sub_n = lax.broadcasted_iota(jnp.int32, (n, cols), 0)
    sub_c = lax.broadcasted_iota(jnp.int32, (cols, cols), 0)
    sub_r = lax.broadcasted_iota(jnp.int32, (rows, cols), 0)
    lane_c = lax.broadcasted_iota(jnp.int32, (cols, cols), 1)
    before = (sub_c < lane_c).astype(jnp.bfloat16)
    offset = lax.rem(me, per) * cap

    def slots(some, carry):
        base, packed_pos = carry
        for r in some:
            hit = (sub_n == target[r : r + 1, :]).astype(jnp.float32)
            onehot_t[r] = hit
            count = jnp.dot(
                hit.astype(jnp.bfloat16), before, preferred_element_type=jnp.float32
            )
            rank = jnp.sum(hit * (count + base), axis=0, keepdims=True).astype(jnp.int32)
            base = base + jnp.sum(hit, axis=1, keepdims=True)
            spread = (sub_c == rank + offset).astype(jnp.bfloat16)
            onehot_r[r] = spread
            onehot_lo[r] = (sub_c == place_lo[r : r + 1, :]).astype(jnp.bfloat16)
            marked = jnp.concatenate(
                [
                    hit * place_hi[r : r + 1, :].astype(jnp.float32),
                    hit * place_lo[r : r + 1, :].astype(jnp.float32),
                ],
                axis=0,
            ).astype(jnp.bfloat16)
            packed_pos = packed_pos + lax.dot_general(
                marked, spread, NT, preferred_element_type=jnp.float32
            )
        return base, packed_pos

    quarter = rows // 4
    sorting = (jnp.zeros((n, 1), jnp.float32), jnp.zeros((2 * n, cols), jnp.float32))
    pivots()
    pl.semaphore_wait(barrier, n - 1)
    for g in range(GROUPS):
        start_halos(0, g)
    sorting = slots(range(quarter), sorting)

    def dynamics(s, g):
        wait_halos(s, g)
        even = lax.rem(lane, 2) == 0
        edges = jnp.where(
            even,
            pltpu.roll(col_from_west[s, g], 1, 1),
            pltpu.roll(col_from_east[s, g], cols - 1, 1),
        )
        part = pl.ds(g * glev, glev)

        def sides(x, p):
            edge = pltpu.roll(edges, lax.rem(cols - 2 * p, cols), 1)
            return (
                jnp.where(at_west, edge, pltpu.roll(x, 1, 1)),
                jnp.where(at_east, edge, pltpu.roll(x, cols - 1, 1)),
            )

        def body(i, packed):
            for j in range(UNROLL):
                r = i * UNROLL + j
                if s == 0:
                    wall_n = jnp.where(
                        jnp.logical_and(r == rows - 1, jnp.logical_not(has_north)), 0.0, 1.0
                    )
                    wall_s = jnp.where(
                        jnp.logical_and(r == 0, jnp.logical_not(has_south)), 0.0, 1.0
                    )
                    m = first[2, r + 1, part]
                    m_s = first[2, r, part]
                    m_n = first[2, r + 2, part]
                    v = first[3, r + 1, part]
                    v_s = first[3, r, part]
                    v_n = first[3, r + 2, part]
                    u = wind[r, part]
                    u_w, u_e = sides(u, 3 * rows + r)
                    m_w, m_e = sides(m, 2 * rows + r)
                    wind_e, mix_e = 0.25 * (u + u_e), 0.5 * (m + m_e)
                    wind_w, mix_w = 0.25 * (u_w + u), 0.5 * (m_w + m)
                    wind_n, mix_n = 0.25 * (v + v_n) * wall_n, 0.5 * (m + m_n) * wall_n
                    wind_s, mix_s = 0.25 * (v_s + v) * wall_s, 0.5 * (m_s + m) * wall_s
                    ce = mix_e - wind_e
                    cw = mix_w + wind_w
                    cn = mix_n - wind_n
                    cs = mix_s + wind_s
                    c0 = (
                        1.0
                        - (wind_e + mix_e)
                        + (wind_w - mix_w)
                        - (wind_n + mix_n)
                        + (wind_s - mix_s)
                    )
                    C0[r, part] = c0
                    CE[r, part] = ce
                    CW[r, part] = cw
                    CN[r, part] = cn
                    CS[r, part] = cs
                else:
                    c0 = C0[r, part]
                    ce = CE[r, part]
                    cw = CW[r, part]
                    cn = CN[r, part]
                    cs = CS[r, part]
                for which in range(2):
                    ref = state(s, which)
                    x = ref[r + 1, part]
                    x_w, x_e = sides(x, which * rows + r)
                    new = (c0 * x + ce * x_e + cw * x_w) + (
                        cn * ref[r + 2, part] + cs * ref[r, part]
                    )
                    if s < NDYN - 1:
                        later[s, which, r + 1, part] = new
                        packed = put(new, which * rows + r, packed)
                    else:
                        (T, Q)[which][pl.ds(pl.multiple_of(r * levels + g * glev, 8), glev), :] = new
            return packed

        packed = lax.fori_loop(0, rows // UNROLL, body, blank)
        if s < NDYN - 1:
            col_out[s + 1, g] = packed
            start_halos(s + 1, g)

    loads[7].wait()
    loads[8].wait()

    def micro(g):
        def body(i, carry):
            for j in range(MICRO // 2):
                r = i * (MICRO // 2) + j
                spots = pl.ds(pl.multiple_of(r * levels + g * glev, 8), glev)
                q0 = Q[spots, :]
                t0 = T[spots, :]
                branch = b_in[pl.ds(g * glev * rows + r, glev, rows), :] > 0
                active = act_in[pl.ds(r, 1), :] > 0
                grow = jnp.where(jnp.logical_and(active, branch), 0.3, 0.0)
                fade = jnp.where(jnp.logical_and(active, jnp.logical_not(branch)), 0.15, 0.0)
                start = GAIN * t0 - 1.0
                q = q0
                condensed = jnp.zeros_like(q0)
                for _ in range(NSUB):
                    saturation = jnp.exp2(start + (2.0 * GAIN) * condensed)
                    excess = q - saturation
                    change = (grow * jnp.maximum(excess, 0.0)) / (1.0 + saturation) + (
                        fade * jnp.minimum(excess, 0.0)
                    )
                    q = q - change
                    condensed = condensed + change
                Q[spots, :] = q
                T[spots, :] = t0 + 2.0 * condensed
                rain[g, pl.ds(r, 1), :] = jnp.sum(condensed, axis=0, keepdims=True)
            return carry

        lax.fori_loop(0, rows // (MICRO // 2), body, 0)

    for s in range(NDYN - 1):
        for g in range(GROUPS):
            dynamics(s, g)
        sorting = slots(range((s + 1) * quarter, (s + 2) * quarter), sorting)
    packed_pos = sorting[1]
    pack2d[:n] = packed_pos[:n] * cols + packed_pos[n:]
    for g in range(GROUPS):
        dynamics(NDYN - 1, g)
        micro(g)
    precip = jnp.sum(rain[...], axis=0) * (4.0 / levels)

    packed = jnp.zeros((3 * n, cols), jnp.float32)
    for r in range(rows):
        packed = packed + lax.dot_general(
            split3(onehot_t[r] * precip[r : r + 1, :]),
            onehot_r[r],
            NT,
            preferred_element_type=jnp.float32,
        )
    pack2d[n:] = join3(packed)

    def packet(i):
        d, dev = peer(i)
        return d, pltpu.make_async_remote_copy(
            src_ref=packet_out.at[d],
            dst_ref=packet_got.at[me],
            send_sem=packet_send.at[d],
            recv_sem=packet_recv.at[me],
            device_id=dev,
            device_id_type=MESH,
        )

    @pl.loop(0, n - 1)
    def _(i):
        d, copy = packet(i)
        packet_out[d, 0:1] = pack2d[pl.ds(d, 1), :]
        packet_out[d, 1:2] = pack2d[pl.ds(n + d, 1), :]
        copy.start()

    packet_got[me] = jnp.zeros(packet_got.shape[1:], jnp.float32)

    def forward(i, carry):
        below, t, q = carry
        for j in range(SOLVE):
            k = i * SOLVE + j
            inverse = INV[level(k), :]
            t = (T[pl.ds(k, rows, levels), :] - below * t) * inverse
            q = (Q[pl.ds(k, rows, levels), :] - below * q) * inverse
            t_in[level(k), :] = t
            q_in[level(k), :] = q
            below = e_in[level(k), :]
        return below, t, q

    lax.fori_loop(0, levels // SOLVE, forward, (plane, plane, plane))

    def backward(i, carry):
        t, q = carry
        for j in range(SOLVE):
            k = levels - 1 - (i * SOLVE + j)
            ratio = RAT[level(k), :]
            t = t_in[level(k), :] - ratio * t
            q = q_in[level(k), :] - ratio * q
            t_out[level(k), :] = t
            q_out[level(k), :] = q
        return t, q

    lax.fori_loop(0, levels // SOLVE, backward, (plane, plane))

    mine = target == me
    collected = jnp.zeros((3 * rows, cols), jnp.float32)
    for r in range(rows):
        keep = jnp.logical_and(mine[r : r + 1, :], sub_r == place_hi[r : r + 1, :])
        collected = collected + lax.dot_general(
            split3(jnp.where(keep, precip[r : r + 1, :], 0.0)),
            onehot_lo[r],
            NT,
            preferred_element_type=jnp.float32,
        )

    @pl.loop(0, n - 1)
    def _(i):
        d = peer(i)[0]
        pltpu.make_async_copy(packet_got.at[d], packet_got.at[d], packet_recv.at[d]).wait()

    for b in range(bundles):
        both = packet_got[b * per]
        for j in range(1, per):
            both = both + packet_got[b * per + j]
        place_b = both[0:1].astype(jnp.int32)
        got_hi = lax.shift_right_logical(place_b, low_shift)
        got_low = (sub_c == (place_b & (cols - 1))).astype(jnp.bfloat16)
        collected = collected + lax.dot_general(
            split3(jnp.where(sub_r == got_hi, both[1:2], 0.0)),
            got_low,
            NT,
            preferred_element_type=jnp.float32,
        )
    g_out[...] = join3(collected)

    for s in range(NDYN):
        for g in range(GROUPS):
            end_halos(s, g)

    @pl.loop(0, n - 1)
    def _(i):
        packet(i)[1].wait_send()


def on_device(t, q, u, v, m, e, b, act, slots):
    nlat = lax.axis_size("lat")
    nlon = lax.axis_size("lon")
    levels, rows, cols = t.shape
    n = nlat * nlon
    glev = levels // GROUPS
    f32 = jnp.float32
    flat = pltpu.VMEM((levels * rows, cols), f32)
    field = pltpu.VMEM((rows, levels, cols), f32)
    column = pltpu.VMEM((NDYN, GROUPS, glev, cols), f32)
    vmem = pl.BlockSpec(memory_space=pltpu.VMEM)
    t_new, q_new, water = pl.pallas_call(
        functools.partial(kernel, nlat, nlon, levels, rows),
        out_shape=(
            jax.ShapeDtypeStruct((levels * rows, cols), f32),
            jax.ShapeDtypeStruct((levels * rows, cols), f32),
            jax.ShapeDtypeStruct((rows, cols), f32),
        ),
        in_specs=[pl.BlockSpec(memory_space=pltpu.HBM)] * 9,
        out_specs=(vmem, vmem, vmem),
        scratch_shapes=[flat] * 6
        + [pltpu.VMEM((levels * rows, cols), jnp.int32)]
        + [pltpu.VMEM((rows, cols), jnp.int32)] * 2
        + [pltpu.SemaphoreType.DMA((9,))]
        + [
            pltpu.VMEM((4, rows + 2, levels, cols), f32),
            pltpu.VMEM((NDYN - 1, 2, rows + 2, levels, cols), f32),
        ]
        + [field] * 6
        + [flat] * 4
        + [column] * 3
        + [
            pltpu.VMEM((GROUPS, rows, cols), f32),
            pltpu.VMEM((rows, n, cols), f32),
            pltpu.VMEM((rows, cols, cols), jnp.bfloat16),
            pltpu.VMEM((rows, cols, cols), jnp.bfloat16),
            pltpu.VMEM((2 * n, cols), f32),
            pltpu.VMEM((n, 2, cols), f32),
            pltpu.VMEM((n, 2, cols), f32),
        ]
        + [pltpu.SemaphoreType.DMA((4, NDYN, GROUPS))] * 2
        + [pltpu.SemaphoreType.DMA((n,))] * 2,
        compiler_params=pltpu.CompilerParams(collective_id=0, has_side_effects=True),
    )(*(x.reshape(levels * rows, cols) for x in (t, q, u, v, m, e, b)), act, slots)
    return t_new.reshape(t.shape), q_new.reshape(t.shape), water.reshape(1, rows * cols)


def solution(mesh):
    grid = P(None, "lat", "lon")
    flat = P("lat", "lon")
    return jax.shard_map(
        on_device,
        mesh=mesh,
        in_specs=(grid,) * 7 + (flat,) * 2,
        out_specs=(grid, grid, P(("lat", "lon"), None)),
        check_vma=False,
    )
```

```python
import functools

import jax
import jax.numpy as jnp
from jax import lax
from jax.experimental import pallas as pl
from jax.experimental.pallas import tpu as pltpu
from jax.sharding import PartitionSpec as P

NDYN = 4
NSUB = 8
GROUPS = 2
UNROLL = 8
MICRO = 8
SOLVE = 8
MESH = pl.DeviceIdType.MESH
LOG2E = 1.4426950408889634
GAIN = 0.25 * LOG2E
NT = (((1,), (1,)), ((), ()))


def split3(x):
    high = x.astype(jnp.bfloat16)
    rest = x - high.astype(jnp.float32)
    mid = rest.astype(jnp.bfloat16)
    low = (rest - mid.astype(jnp.float32)).astype(jnp.bfloat16)
    return jnp.concatenate([high, mid, low], axis=0)


def join3(x):
    n = x.shape[0] // 3
    return x[:n] + x[n : 2 * n] + x[2 * n :]


def kernel(
    nlat,
    nlon,
    levels,
    rows,
    t_hbm,
    q_hbm,
    u_hbm,
    v_hbm,
    m_hbm,
    e_hbm,
    b_hbm,
    act_hbm,
    map_hbm,
    t_out,
    q_out,
    g_out,
    t_in,
    q_in,
    u_in,
    v_in,
    m_in,
    e_in,
    b_in,
    act_in,
    map_in,
    load_sem,
    first,
    later,
    wind,
    C0,
    CE,
    CW,
    CN,
    CS,
    T,
    Q,
    INV,
    RAT,
    col_out,
    col_from_west,
    col_from_east,
    rain,
    onehot_t,
    onehot_r,
    onehot_lo,
    pack2d,
    packet_out,
    packet_got,
    halo_send,
    halo_recv,
    packet_send,
    packet_recv,
):
    cols = t_hbm.shape[1]
    n = nlat * nlon
    width = rows * cols
    cap = width // (2 * n)
    per = cols // cap
    bundles = n // per
    glev = levels // GROUPS
    lat = lax.axis_index("lat")
    lon = lax.axis_index("lon")
    me = lat * nlon + lon
    east = lax.rem(lon + 1, nlon)
    west = lax.rem(lon + nlon - 1, nlon)
    north = lax.rem(lat + 1, nlat)
    south = lax.rem(lat + nlat - 1, nlat)
    has_north = lat < nlat - 1
    has_south = lat > 0

    def peer(i):
        d = lax.rem(me + 1 + i, n)
        return d, (d // nlon, lax.rem(d, nlon))

    loads = {}
    for i, (source, held) in enumerate(
        (
            (t_hbm, t_in),
            (q_hbm, q_in),
            (m_hbm, m_in),
            (u_hbm, u_in),
            (v_hbm, v_in),
            (map_hbm, map_in),
            (e_hbm, e_in),
            (act_hbm, act_in),
            (b_hbm, b_in),
        )
    ):
        loads[i] = pltpu.make_async_copy(source, held, load_sem.at[i])
        loads[i].start()

    barrier = pltpu.get_barrier_semaphore()

    @pl.loop(0, n - 1)
    def _(i):
        pl.semaphore_signal(barrier, inc=1, device_id=peer(i)[1], device_id_type=MESH)

    def state(s, which):
        return first.at[which] if s == 0 else later.at[s - 1, which]

    def halo(kind, s, g):
        part = pl.ds(g * glev, glev)
        if kind == 0:
            src, dst, dev = col_out.at[s, g], col_from_west.at[s, g], (lat, east)
        elif kind == 1:
            src, dst, dev = col_out.at[s, g], col_from_east.at[s, g], (lat, west)
        else:
            ref = first if s == 0 else later.at[s - 1]
            source, target, y = (rows, 0, north) if kind == 2 else (1, rows + 1, south)
            src, dst, dev = ref.at[:, source, part], ref.at[:, target, part], (y, lon)
        return pltpu.make_async_remote_copy(
            src_ref=src,
            dst_ref=dst,
            send_sem=halo_send.at[kind, s, g],
            recv_sem=halo_recv.at[kind, s, g],
            device_id=dev,
            device_id_type=MESH,
        )

    def start_halos(s, g):
        pl.when(has_north)(lambda: halo(2, s, g).start())
        pl.when(has_south)(lambda: halo(3, s, g).start())
        halo(0, s, g).start()
        halo(1, s, g).start()

    def wait_halos(s, g):
        halo(0, s, g).wait_recv()
        halo(1, s, g).wait_recv()
        pl.when(has_south)(lambda: halo(2, s, g).wait_recv())
        pl.when(has_north)(lambda: halo(3, s, g).wait_recv())

    def end_halos(s, g):
        halo(0, s, g).wait_send()
        halo(1, s, g).wait_send()
        pl.when(has_north)(lambda: halo(2, s, g).wait_send())
        pl.when(has_south)(lambda: halo(3, s, g).wait_send())

    lane = lax.broadcasted_iota(jnp.int32, (glev, cols), 1)
    pair = (lane + 1) // 2
    pair = jnp.where(lane == cols - 1, 0, pair)
    at_west = lane == 0
    at_east = lane == cols - 1

    def put(x, p, packed):
        return jnp.where(pair == p, pltpu.roll(x, 2 * p, 1), packed)

    blank = jnp.zeros((glev, cols), jnp.float32)

    @pl.when(jnp.logical_not(has_north))
    def _():
        first[:, rows + 1] = jnp.zeros_like(first[:, rows + 1])
        later[:, :, rows + 1] = jnp.zeros_like(later[:, :, rows + 1])

    @pl.when(jnp.logical_not(has_south))
    def _():
        first[:, 0] = jnp.zeros_like(first[:, 0])
        later[:, :, 0] = jnp.zeros_like(later[:, :, 0])

    for i in range(5):
        loads[i].wait()

    for g in range(GROUPS):

        def arrange(i, packed, g=g):
            for j in range(UNROLL):
                r = i * UNROLL + j
                spots = pl.ds(g * glev * rows + r, glev, rows)
                part = pl.ds(g * glev, glev)
                for which, ref in enumerate((t_in, q_in, m_in)):
                    x = ref[spots, :]
                    first[which, r + 1, part] = x
                    packed = put(x, which * rows + r, packed)
                x = u_in[spots, :]
                wind[r, part] = x
                packed = put(x, 3 * rows + r, packed)
                first[3, r + 1, part] = v_in[spots, :]
            return packed

        col_out[0, g] = lax.fori_loop(0, rows // UNROLL, arrange, blank)

    loads[6].wait()
    plane = jnp.zeros((rows, cols), jnp.float32)

    def level(k):
        return pl.ds(pl.multiple_of(k * rows, rows), rows)

    def pivot_body(i, carry):
        below, ratio = carry
        for j in range(SOLVE):
            k = i * SOLVE + j
            above = jnp.where(k < levels - 1, e_in[level(k), :], 0.0)
            inverse = 1.0 / (1.0 + below + above - below * ratio)
            ratio = above * inverse
            INV[level(k), :] = inverse
            RAT[level(k), :] = ratio
            below = above
        return below, ratio

    def pivots():
        lax.fori_loop(0, levels // SOLVE, pivot_body, (plane, plane))

    loads[5].wait()
    shift = width.bit_length() - 1
    low_shift = cols.bit_length() - 1
    slot = map_in[...]
    target = lax.shift_right_logical(slot, shift)
    place = slot & (width - 1)
    place_hi = lax.shift_right_logical(place, low_shift)
    place_lo = place & (cols - 1)
    sub_n = lax.broadcasted_iota(jnp.int32, (n, cols), 0)
    sub_c = lax.broadcasted_iota(jnp.int32, (cols, cols), 0)
    sub_r = lax.broadcasted_iota(jnp.int32, (rows, cols), 0)
    lane_c = lax.broadcasted_iota(jnp.int32, (cols, cols), 1)
    before = (sub_c < lane_c).astype(jnp.bfloat16)
    offset = lax.rem(me, per) * cap

    def slots(some, carry):
        base, packed_pos = carry
        for r in some:
            hit = (sub_n == target[r : r + 1, :]).astype(jnp.float32)
            onehot_t[r] = hit
            count = jnp.dot(
                hit.astype(jnp.bfloat16), before, preferred_element_type=jnp.float32
            )
            rank = jnp.sum(hit * (count + base), axis=0, keepdims=True).astype(jnp.int32)
            base = base + jnp.sum(hit, axis=1, keepdims=True)
            spread = (sub_c == rank + offset).astype(jnp.bfloat16)
            onehot_r[r] = spread
            onehot_lo[r] = (sub_c == place_lo[r : r + 1, :]).astype(jnp.bfloat16)
            marked = jnp.concatenate(
                [
                    hit * place_hi[r : r + 1, :].astype(jnp.float32),
                    hit * place_lo[r : r + 1, :].astype(jnp.float32),
                ],
                axis=0,
            ).astype(jnp.bfloat16)
            packed_pos = packed_pos + lax.dot_general(
                marked, spread, NT, preferred_element_type=jnp.float32
            )
        return base, packed_pos

    quarter = rows // 4
    sorting = (jnp.zeros((n, 1), jnp.float32), jnp.zeros((2 * n, cols), jnp.float32))
    pivots()
    pl.semaphore_wait(barrier, n - 1)
    for g in range(GROUPS):
        start_halos(0, g)
    sorting = slots(range(quarter), sorting)

    def dynamics(s, g):
        wait_halos(s, g)
        even = lax.rem(lane, 2) == 0
        edges = jnp.where(
            even,
            pltpu.roll(col_from_west[s, g], 1, 1),
            pltpu.roll(col_from_east[s, g], cols - 1, 1),
        )
        part = pl.ds(g * glev, glev)

        def sides(x, p):
            edge = pltpu.roll(edges, lax.rem(cols - 2 * p, cols), 1)
            return (
                jnp.where(at_west, edge, pltpu.roll(x, 1, 1)),
                jnp.where(at_east, edge, pltpu.roll(x, cols - 1, 1)),
            )

        def body(i, packed):
            for j in range(UNROLL):
                r = i * UNROLL + j
                if s == 0:
                    wall_n = jnp.where(
                        jnp.logical_and(r == rows - 1, jnp.logical_not(has_north)), 0.0, 1.0
                    )
                    wall_s = jnp.where(
                        jnp.logical_and(r == 0, jnp.logical_not(has_south)), 0.0, 1.0
                    )
                    m = first[2, r + 1, part]
                    m_s = first[2, r, part]
                    m_n = first[2, r + 2, part]
                    v = first[3, r + 1, part]
                    v_s = first[3, r, part]
                    v_n = first[3, r + 2, part]
                    u = wind[r, part]
                    u_w, u_e = sides(u, 3 * rows + r)
                    m_w, m_e = sides(m, 2 * rows + r)
                    wind_e, mix_e = 0.25 * (u + u_e), 0.5 * (m + m_e)
                    wind_w, mix_w = 0.25 * (u_w + u), 0.5 * (m_w + m)
                    wind_n, mix_n = 0.25 * (v + v_n) * wall_n, 0.5 * (m + m_n) * wall_n
                    wind_s, mix_s = 0.25 * (v_s + v) * wall_s, 0.5 * (m_s + m) * wall_s
                    ce = mix_e - wind_e
                    cw = mix_w + wind_w
                    cn = mix_n - wind_n
                    cs = mix_s + wind_s
                    c0 = (
                        1.0
                        - (wind_e + mix_e)
                        + (wind_w - mix_w)
                        - (wind_n + mix_n)
                        + (wind_s - mix_s)
                    )
                    C0[r, part] = c0
                    CE[r, part] = ce
                    CW[r, part] = cw
                    CN[r, part] = cn
                    CS[r, part] = cs
                else:
                    c0 = C0[r, part]
                    ce = CE[r, part]
                    cw = CW[r, part]
                    cn = CN[r, part]
                    cs = CS[r, part]
                for which in range(2):
                    ref = state(s, which)
                    x = ref[r + 1, part]
                    x_w, x_e = sides(x, which * rows + r)
                    new = (c0 * x + ce * x_e + cw * x_w) + (
                        cn * ref[r + 2, part] + cs * ref[r, part]
                    )
                    if s < NDYN - 1:
                        later[s, which, r + 1, part] = new
                        packed = put(new, which * rows + r, packed)
                    else:
                        (T, Q)[which][pl.ds(pl.multiple_of(r * levels + g * glev, 8), glev), :] = new
            return packed

        packed = lax.fori_loop(0, rows // UNROLL, body, blank)
        if s < NDYN - 1:
            col_out[s + 1, g] = packed
            start_halos(s + 1, g)

    loads[7].wait()
    loads[8].wait()

    def micro(g):
        def body(i, carry):
            for j in range(MICRO // 2):
                r = i * (MICRO // 2) + j
                spots = pl.ds(pl.multiple_of(r * levels + g * glev, 8), glev)
                q0 = Q[spots, :]
                t0 = T[spots, :]
                branch = b_in[pl.ds(g * glev * rows + r, glev, rows), :] > 0
                active = act_in[pl.ds(r, 1), :] > 0
                grow = jnp.where(jnp.logical_and(active, branch), 0.3, 0.0)
                fade = jnp.where(jnp.logical_and(active, jnp.logical_not(branch)), 0.15, 0.0)
                start = GAIN * t0 - 1.0
                q = q0
                condensed = jnp.zeros_like(q0)
                for _ in range(NSUB):
                    saturation = jnp.exp2(start + (2.0 * GAIN) * condensed)
                    excess = q - saturation
                    change = (grow * jnp.maximum(excess, 0.0)) / (1.0 + saturation) + (
                        fade * jnp.minimum(excess, 0.0)
                    )
                    q = q - change
                    condensed = condensed + change
                Q[spots, :] = q
                T[spots, :] = t0 + 2.0 * condensed
                rain[g, pl.ds(r, 1), :] = jnp.sum(condensed, axis=0, keepdims=True)
            return carry

        lax.fori_loop(0, rows // (MICRO // 2), body, 0)

    for s in range(NDYN - 1):
        for g in range(GROUPS):
            dynamics(s, g)
        sorting = slots(range((s + 1) * quarter, (s + 2) * quarter), sorting)
    packed_pos = sorting[1]
    pack2d[:n] = packed_pos[:n] * cols + packed_pos[n:]
    for g in range(GROUPS):
        dynamics(NDYN - 1, g)
        micro(g)
    precip = jnp.sum(rain[...], axis=0) * (4.0 / levels)

    packed = jnp.zeros((3 * n, cols), jnp.float32)
    for r in range(rows):
        packed = packed + lax.dot_general(
            split3(onehot_t[r] * precip[r : r + 1, :]),
            onehot_r[r],
            NT,
            preferred_element_type=jnp.float32,
        )
    pack2d[n:] = join3(packed)

    def packet(i):
        d, dev = peer(i)
        return d, pltpu.make_async_remote_copy(
            src_ref=packet_out.at[d],
            dst_ref=packet_got.at[me],
            send_sem=packet_send.at[d],
            recv_sem=packet_recv.at[me],
            device_id=dev,
            device_id_type=MESH,
        )

    @pl.loop(0, n - 1)
    def _(i):
        d, copy = packet(i)
        packet_out[d, 0:1] = pack2d[pl.ds(d, 1), :]
        packet_out[d, 1:2] = pack2d[pl.ds(n + d, 1), :]
        copy.start()

    packet_got[me] = jnp.zeros(packet_got.shape[1:], jnp.float32)

    def forward(i, carry):
        below, t, q = carry
        for j in range(SOLVE):
            k = i * SOLVE + j
            inverse = INV[level(k), :]
            t = (T[pl.ds(k, rows, levels), :] - below * t) * inverse
            q = (Q[pl.ds(k, rows, levels), :] - below * q) * inverse
            t_in[level(k), :] = t
            q_in[level(k), :] = q
            below = e_in[level(k), :]
        return below, t, q

    lax.fori_loop(0, levels // SOLVE, forward, (plane, plane, plane))

    def backward(i, carry):
        t, q = carry
        for j in range(SOLVE):
            k = levels - 1 - (i * SOLVE + j)
            ratio = RAT[level(k), :]
            t = t_in[level(k), :] - ratio * t
            q = q_in[level(k), :] - ratio * q
            t_out[level(k), :] = t
            q_out[level(k), :] = q
        return t, q

    lax.fori_loop(0, levels // SOLVE, backward, (plane, plane))

    mine = target == me
    collected = jnp.zeros((3 * rows, cols), jnp.float32)
    for r in range(rows):
        keep = jnp.logical_and(mine[r : r + 1, :], sub_r == place_hi[r : r + 1, :])
        collected = collected + lax.dot_general(
            split3(jnp.where(keep, precip[r : r + 1, :], 0.0)),
            onehot_lo[r],
            NT,
            preferred_element_type=jnp.float32,
        )

    @pl.loop(0, n - 1)
    def _(i):
        d = peer(i)[0]
        pltpu.make_async_copy(packet_got.at[d], packet_got.at[d], packet_recv.at[d]).wait()

    for b in range(bundles):
        both = packet_got[b * per]
        for j in range(1, per):
            both = both + packet_got[b * per + j]
        place_b = both[0:1].astype(jnp.int32)
        got_hi = lax.shift_right_logical(place_b, low_shift)
        got_low = (sub_c == (place_b & (cols - 1))).astype(jnp.bfloat16)
        collected = collected + lax.dot_general(
            split3(jnp.where(sub_r == got_hi, both[1:2], 0.0)),
            got_low,
            NT,
            preferred_element_type=jnp.float32,
        )
    g_out[...] = join3(collected)

    for s in range(NDYN):
        for g in range(GROUPS):
            end_halos(s, g)

    @pl.loop(0, n - 1)
    def _(i):
        packet(i)[1].wait_send()


def on_device(t, q, u, v, m, e, b, act, slots):
    nlat = lax.axis_size("lat")
    nlon = lax.axis_size("lon")
    levels, rows, cols = t.shape
    n = nlat * nlon
    glev = levels // GROUPS
    f32 = jnp.float32
    flat = pltpu.VMEM((levels * rows, cols), f32)
    field = pltpu.VMEM((rows, levels, cols), f32)
    column = pltpu.VMEM((NDYN, GROUPS, glev, cols), f32)
    vmem = pl.BlockSpec(memory_space=pltpu.VMEM)
    t_new, q_new, water = pl.pallas_call(
        functools.partial(kernel, nlat, nlon, levels, rows),
        out_shape=(
            jax.ShapeDtypeStruct((levels * rows, cols), f32),
            jax.ShapeDtypeStruct((levels * rows, cols), f32),
            jax.ShapeDtypeStruct((rows, cols), f32),
        ),
        in_specs=[pl.BlockSpec(memory_space=pltpu.HBM)] * 9,
        out_specs=(vmem, vmem, vmem),
        scratch_shapes=[flat] * 6
        + [pltpu.VMEM((levels * rows, cols), jnp.int32)]
        + [pltpu.VMEM((rows, cols), jnp.int32)] * 2
        + [pltpu.SemaphoreType.DMA((9,))]
        + [
            pltpu.VMEM((4, rows + 2, levels, cols), f32),
            pltpu.VMEM((NDYN - 1, 2, rows + 2, levels, cols), f32),
        ]
        + [field] * 6
        + [flat] * 4
        + [column] * 3
        + [
            pltpu.VMEM((GROUPS, rows, cols), f32),
            pltpu.VMEM((rows, n, cols), f32),
            pltpu.VMEM((rows, cols, cols), jnp.bfloat16),
            pltpu.VMEM((rows, cols, cols), jnp.bfloat16),
            pltpu.VMEM((2 * n, cols), f32),
            pltpu.VMEM((n, 2, cols), f32),
            pltpu.VMEM((n, 2, cols), f32),
        ]
        + [pltpu.SemaphoreType.DMA((4, NDYN, GROUPS))] * 2
        + [pltpu.SemaphoreType.DMA((n,))] * 2,
        compiler_params=pltpu.CompilerParams(collective_id=0, has_side_effects=True),
    )(*(x.reshape(levels * rows, cols) for x in (t, q, u, v, m, e, b)), act, slots)
    return t_new.reshape(t.shape), q_new.reshape(t.shape), water.reshape(1, rows * cols)


def solution(mesh):
    grid = P(None, "lat", "lon")
    flat = P("lat", "lon")
    return jax.shard_map(
        on_device,
        mesh=mesh,
        in_specs=(grid,) * 7 + (flat,) * 2,
        out_specs=(grid, grid, P(("lat", "lon"), None)),
        check_vma=False,
    )
```
